32 devices in a mesh: row: 4 (over y, x), col: 8 (over z, core).
Axes of the slice: x: 2, y: 2, z: 4, core: 2. Of those that a mesh axis runs over, the one named last changes fastest.
Arguments:
- stream_in: bfloat16 [1024, 8192], P('col', 'row'), may hold values from -6 to 6
- grad_out: bfloat16 [1024, 8192], P('col', 'row'), may hold values from -6 to 6
- gate_pre: bfloat16 [1024, 14336], P('row', 'col'), may hold values from -6 to 6
- up_pre: bfloat16 [1024, 14336], P('row', 'col'), may hold values from -6 to 6
- keep_mask: int32 [1024, 14336], P('row', 'col'), may hold values 0 or 1
- segment_ids: int32 [1024], P('row'), may hold values from 0 to 15, never falling along the last dimension, each value on 1 to 128 neighbouring positions
- norm_gain: float32 [8192], P('row'), may hold values from 0.25 to 1.75
- w_gate: bfloat16 [8192, 14336], P('row', 'col'), may hold values from -0.0625 to 0.0625
- w_up: bfloat16 [8192, 14336], P('row', 'col'), may hold values from -0.0625 to 0.0625
- w_down: bfloat16 [14336, 8192], P('col', 'row'), may hold values from -0.046875 to 0.046875
Outputs:
- grad_in: bfloat16 [1024, 8192], P('col', 'row')
- grad_gate: bfloat16 [8192, 14336], P('row', 'col')
- grad_up: bfloat16 [8192, 14336], P('row', 'col')
- grad_down: bfloat16 [14336, 8192], P('col', 'row')
The draws below stay inside these ranges and needn't reach their ends.
Inputs may be any that keep to these rules, and one draw needn't show every extreme that they name: `segment_ids`: never falls along the tokens; each of the 16 documents has 1 to 128 tokens, one exactly 128.
All inputs are finite; a program needn't handle non-finite values. No bound on the sum of `keep_mask` on one device may be relied on, other than what follows from the above.
Results may differ from the reference program's by a relative error of at most 0.0059.
Values may be sent and summed in bfloat16 or wider, within the bound.
No kernel may reach another device: no remote copies, remote signals or barrier semaphores. Data moves between devices by JAX's collectives and lax.ppermute only.
A program may use at most 128 MiB of HBM per device.

```python
import math
import jax
import jax.numpy as jnp
import numpy as np
from jax import lax

D = 8192
FF = 14336
SEGS = 16
TOKENS = 1024
MOST = 128


def touch_ends(values, rng, low, high):
    extent = values.shape
    spot = [jax.random.randint(jax.random.fold_in(rng, axis), (), 0, extent[axis]) for axis in range(len(extent))]
    values = values.at[tuple(spot)].set(low)
    longest = extent.index(max(extent))
    spot[longest] = (spot[longest] + 1) % extent[longest]
    return values.at[tuple(spot)].set(high)


def shard_levels(key, shape, split, low, high):
    level = 1.0
    for position, blocks in split:
        heights = jax.random.uniform(jax.random.fold_in(jax.random.fold_in(key, 6), position), (blocks,), jnp.float32, low / len(split), high / len(split))
        level = level * jnp.repeat(jnp.exp(heights), shape[position] // blocks).reshape((-1,) + (1,) * (len(shape) - 1 - position))
    return level


def length_profile(count, total, limit, lean):
    portions = [(1 << 20) // math.isqrt(standing ** lean) + 1 for standing in range(2, count + 1)]
    spare, given = total - limit - (count - 1), [1] * (count - 1)
    while spare > 0:
        movable = [i for i in range(count - 1) if given[i] < limit]
        pool, remaining = sum([portions[i] for i in movable]), spare
        for i in movable:
            extra = min(limit - given[i], max(1, remaining * portions[i] // pool), spare)
            given[i] = given[i] + extra
            spare = spare - extra
    return np.array([limit] + given)


def ragged_sizes(key, number_of, total, reach, lean):
    if number_of == 2:
        one = jax.random.randint(key, (), max(1, total - reach), min(reach, total - 1) + 1)
        return jnp.stack([one, total - one])
    lengths = jnp.asarray(length_profile(number_of, total, reach, lean), jnp.int32)
    couples = (number_of - 1) // 2
    source_of, sink = lengths[1:1 + 2 * couples:2], lengths[2:2 + 2 * couples:2]
    margin = jnp.minimum(source_of - 1, reach - sink)
    shifted = jax.random.randint(jax.random.fold_in(key, 1), (couples,), 0, 1 << 20) % (margin + 1)
    lengths = lengths.at[1:1 + 2 * couples:2].set(source_of - shifted).at[2:2 + 2 * couples:2].set(sink + shifted)
    return lengths[jax.random.permutation(jax.random.fold_in(key, 2), number_of)]


def gaussian(own_key, extent, width, limit, shards=(), kind=jnp.bfloat16):
    array = jax.random.normal(own_key, extent, jnp.float32) * width
    if len(shards) > 0:
        array = shard_levels(own_key, extent, shards, -0.22, 0.18) * array
    return jnp.clip(array, min=-limit, max=limit).astype(kind)


def setup_inputs(seed: int = 0) -> dict:
    key_list = jax.random.split(jax.random.key(seed), 11)
    return {
        "stream_in": gaussian(key_list[0], (TOKENS, D), 1.0, 6.0, ((0, 8), (1, 4))),
        "grad_out": gaussian(key_list[1], (TOKENS, D), 1.0, 6.0, ((0, 8), (1, 4))),
        "gate_pre": gaussian(key_list[2], (TOKENS, FF), 1.5, 6.0, ((0, 4), (1, 8))),
        "up_pre": gaussian(key_list[3], (TOKENS, FF), 1.0, 6.0, ((0, 4), (1, 8))),
        "keep_mask": touch_ends((jax.random.randint(key_list[4], (TOKENS, FF), 0, 10) < 9).astype(jnp.int32), jax.random.fold_in(key_list[4], 1), 0, 1),
        "segment_ids": jnp.searchsorted(jnp.cumsum(ragged_sizes(key_list[5], SEGS, TOKENS, MOST, 1)), jnp.arange(TOKENS), side="right").astype(jnp.int32),
        "norm_gain": jnp.clip(1.0 + 0.15 * jax.random.normal(key_list[6], (D,), jnp.float32), 0.25, 1.75),
        "w_gate": gaussian(key_list[7], (D, FF), D ** -0.5, 0.0625, ((0, 4), (1, 8))),
        "w_up": gaussian(key_list[8], (D, FF), D ** -0.5, 0.0625, ((0, 4), (1, 8))),
        "w_down": gaussian(key_list[9], (FF, D), FF ** -0.5, 0.046875, ((0, 8), (1, 4))),
    }


eps = 1e-05
keep_scale = 1.0 / 0.9

def reference(stream_in, grad_out, gate_pre, up_pre, keep_mask, segment_ids, norm_gain, w_gate, w_up, w_down):
    xs = stream_in.astype(jnp.float32)
    onehot = (segment_ids[:, None] == jnp.arange(SEGS, dtype=jnp.int32)[None, :]).astype(jnp.float32)
    counts = lax.optimization_barrier(jnp.sum(onehot, axis=0))
    weights = lax.optimization_barrier(jnp.sum(onehot * (TOKENS / (SEGS * counts))[None, :], axis=1))
    recip = lax.rsqrt(lax.optimization_barrier(jnp.sum(xs * xs, axis=1)) / D + eps)
    normed = (xs * recip[:, None] * norm_gain[None, :]).astype(jnp.bfloat16)
    gate_f = gate_pre.astype(jnp.float32)
    up_f = up_pre.astype(jnp.float32)
    sig = jax.nn.sigmoid(gate_f)
    keep_f = keep_mask.astype(jnp.float32) * keep_scale
    dropped = (gate_f * sig * up_f * keep_f * weights[:, None]).astype(jnp.bfloat16)
    back = jnp.dot(grad_out, w_down.T, preferred_element_type=jnp.float32)
    grad_act = back * weights[:, None] * keep_f
    grad_gpre = (grad_act * up_f * sig * (1.0 + gate_f * (1.0 - sig))).astype(jnp.bfloat16)
    grad_upre = (grad_act * gate_f * sig).astype(jnp.bfloat16)
    grad_down = jnp.dot(dropped.T, grad_out, preferred_element_type=jnp.float32).astype(jnp.bfloat16)
    grad_gate = jnp.dot(normed.T, grad_gpre, preferred_element_type=jnp.float32).astype(jnp.bfloat16)
    grad_up = jnp.dot(normed.T, grad_upre, preferred_element_type=jnp.float32).astype(jnp.bfloat16)
    grad_normed = jnp.dot(grad_gpre, w_gate.T, preferred_element_type=jnp.float32) + jnp.dot(grad_upre, w_up.T, preferred_element_type=jnp.float32)
    scaled = grad_normed * norm_gain[None, :]
    inner = lax.optimization_barrier(jnp.sum(scaled * xs, axis=1)) / D
    branch = recip[:, None] * (scaled - xs * (recip * recip * inner)[:, None])
    grad_in = (grad_out.astype(jnp.float32) + branch).astype(jnp.bfloat16)
    return (grad_in, grad_gate, grad_up, grad_down)
```

```python
import functools

import jax
import jax.numpy as jnp
from jax import lax
from jax.experimental import pallas as pl
from jax.experimental.pallas import tpu as pltpu
from jax.sharding import PartitionSpec as P

D = 8192
SEGS = 16
CHUNKS = 2

eps = 1e-05
keep_scale = 1.0 / 0.9
bf16 = jnp.bfloat16
f32 = jnp.float32
ANY = pl.BlockSpec(memory_space=pl.ANY)


def over_tokens(left, right):
    return lax.dot_general(left, right, (((0,), (0,)), ((), ())), preferred_element_type=f32)


def over_width(left, right):
    return lax.dot_general(left, right, (((1,), (1,)), ((), ())), preferred_element_type=f32)


def join_kernel(n, *refs):
    parts, out, sems = refs[:n], refs[-2], refs[-1]
    copies = [pltpu.make_async_copy(parts[s], out.at[s], sems.at[s]) for s in range(n)]
    for copy in copies:
        copy.start()
    for copy in copies:
        copy.wait()


def join(parts, after=()):
    n = len(parts)
    shape = (n,) + parts[0].shape
    return pl.pallas_call(
        functools.partial(join_kernel, n),
        out_shape=jax.ShapeDtypeStruct(shape, parts[0].dtype),
        in_specs=[ANY] * (n + len(after)),
        scratch_shapes=[pltpu.SemaphoreType.DMA((n,))],
        compiler_params=pltpu.CompilerParams(vmem_limit_bytes=32 * 1024 * 1024),
        cost_estimate=pl.CostEstimate(
            flops=0, bytes_accessed=4 * n * parts[0].size, transcendentals=0
        ),
    )(*parts, *after)


def fill(n, where, mine, other, out, sems):
    core = where[0]
    copies = []
    for s in range(n):
        copies.append(pltpu.make_async_copy(mine.at[s], out.at[where[1 + s], core], sems.at[s]))
        copies.append(
            pltpu.make_async_copy(other.at[s], out.at[where[1 + s], 1 - core], sems.at[n + s])
        )
    for copy in copies:
        copy.start()
    for copy in copies:
        copy.wait()


def place_kernel(n, where, mine, other, *refs):
    fill(n, where, mine, other, refs[-2], refs[-1])


def place(where, mine, other, after=()):
    n, shape = mine.shape[0], mine.shape[1:]
    return pl.pallas_call(
        functools.partial(place_kernel, n),
        out_shape=jax.ShapeDtypeStruct((n, 2) + shape, mine.dtype),
        in_specs=[pl.BlockSpec(memory_space=pltpu.SMEM)] + [ANY] * (2 + len(after)),
        scratch_shapes=[pltpu.SemaphoreType.DMA((2 * n,))],
        compiler_params=pltpu.CompilerParams(vmem_limit_bytes=32 * 1024 * 1024),
        cost_estimate=pl.CostEstimate(flops=0, bytes_accessed=8 * mine.size, transcendentals=0),
    )(where, mine, other, *after)


def back_kernel(n, where, mine, other, w_ref, *refs):
    cot, part, sems = refs[-3:]

    @pl.when(pl.program_id(0) == 0)
    def _():
        fill(n, where, mine, other, cot, sems)

    left = cot[...].reshape(-1, cot.shape[-1])
    out = over_width(left, w_ref[...]).astype(bf16)
    part[...] = out.reshape(part.shape)


def back(where, mine, other, w_down, after=()):
    n, sub, feat = mine.shape
    width = w_down.shape[0]
    tile = width // 2 if width // 2 % 128 == 0 else width
    tokens = 2 * n * sub
    return pl.pallas_call(
        functools.partial(back_kernel, n),
        out_shape=(
            jax.ShapeDtypeStruct((n, 2, sub, feat), bf16),
            jax.ShapeDtypeStruct((n, 2 * sub, width), bf16),
        ),
        grid=(width // tile,),
        in_specs=[
            pl.BlockSpec(memory_space=pltpu.SMEM),
            ANY,
            ANY,
            pl.BlockSpec((tile, feat), lambda i: (i, 0)),
        ]
        + [ANY] * len(after),
        out_specs=(
            pl.BlockSpec((n, 2, sub, feat), lambda i: (0, 0, 0, 0)),
            pl.BlockSpec((n, 2 * sub, tile), lambda i: (0, 0, i)),
        ),
        scratch_shapes=[pltpu.SemaphoreType.DMA((2 * n,))],
        compiler_params=pltpu.CompilerParams(vmem_limit_bytes=48 * 1024 * 1024),
        cost_estimate=pl.CostEstimate(
            flops=2 * tokens * width * feat,
            bytes_accessed=2 * (2 * tokens * feat + width * feat + tokens * width),
            transcendentals=0,
        ),
    )(where, mine, other, w_down, *after)


def dropped_kernel(gate_ref, up_ref, keep_ref, weight_ref, *refs):
    out = refs[-1]
    for k in range(CHUNKS):
        gate = gate_ref[:, k].astype(f32)
        scale = keep_ref[:, k].astype(f32) * keep_scale * weight_ref[:, k]
        value = gate * jax.nn.sigmoid(gate) * up_ref[:, k].astype(f32) * scale
        out[k] = value.astype(bf16).reshape(out.shape[1:])


def masked(gate, up, keep, weights):
    two, chunks, sub, width = gate.shape
    tile = 256 if width % 256 == 0 else 128
    block = pl.BlockSpec((two, chunks, sub, tile), lambda i: (0, 0, 0, i))
    return pl.pallas_call(
        dropped_kernel,
        out_shape=jax.ShapeDtypeStruct((chunks, two * sub, width), bf16),
        grid=(width // tile,),
        in_specs=[
            block,
            block,
            block,
            pl.BlockSpec((two, chunks, sub, 1), lambda i: (0, 0, 0, 0)),
        ],
        out_specs=pl.BlockSpec((chunks, two * sub, tile), lambda i: (0, 0, i)),
        cost_estimate=pl.CostEstimate(
            flops=10 * gate.size, bytes_accessed=10 * gate.size, transcendentals=gate.size
        ),
    )(gate, up, keep, weights)


def grads_kernel(n, *refs):
    own, parts = refs[0], refs[1:n]
    gate_ref, up_ref, keep_ref, weight_ref = refs[n : n + 4]
    out = refs[-1]
    total = own[0].astype(f32)
    for part in parts:
        total = total + part[...].astype(f32)
    two, sub, tile = gate_ref.shape
    total = total.reshape(two, sub, tile)
    gate, up = gate_ref[...].astype(f32), up_ref[...].astype(f32)
    act = total * (keep_ref[...].astype(f32) * keep_scale * weight_ref[...])
    sig = jax.nn.sigmoid(gate)
    out[0] = (act * up * sig * (1.0 + gate * (1.0 - sig))).astype(bf16).reshape(out.shape[1:])
    out[1] = (act * gate * sig).astype(bf16).reshape(out.shape[1:])


def hidden_grads(k, own, parts, gate, up, keep, weights, after=()):
    n = 1 + len(parts)
    two, chunks, sub, width = gate.shape
    tile = 256 if width % 256 == 0 else 128
    block = pl.BlockSpec((two, None, sub, tile), lambda i: (0, k, 0, i))
    size = two * sub * width
    return pl.pallas_call(
        functools.partial(grads_kernel, n),
        out_shape=jax.ShapeDtypeStruct((2, two * sub, width), bf16),
        grid=(width // tile,),
        in_specs=[pl.BlockSpec((1, two * sub, tile), lambda i: (0, 0, i))]
        + [pl.BlockSpec((two * sub, tile), lambda i: (0, i))] * (n - 1)
        + [block] * 3
        + [pl.BlockSpec((two, None, sub, 1), lambda i: (0, k, 0, 0))]
        + [ANY] * len(after),
        out_specs=pl.BlockSpec((2, two * sub, tile), lambda i: (0, 0, i)),
        cost_estimate=pl.CostEstimate(
            flops=20 * size, bytes_accessed=(12 + 2 * n) * size, transcendentals=size
        ),
    )(own, *parts, gate, up, keep, weights, *after)


def hidden_kernel(n, where_ref, gpre_ref, upre_ref, wg_ref, wu_ref, *refs):
    give_ref, keep_ref = refs[-2:]
    core = where_ref[0]
    shift = where_ref[1]
    part = over_width(gpre_ref[...], wg_ref[...]) + over_width(upre_ref[...], wu_ref[...])
    sub = give_ref.shape[1]
    part = part.reshape(n, 2, sub, part.shape[1])
    low = core == 0
    for j in range(n):
        at = lax.bitwise_xor(shift, j)
        keep_ref[at] = jnp.where(low, part[j, 0], part[j, 1])
        give_ref[at] = jnp.where(low, part[j, 1], part[j, 0]).astype(bf16)


def hidden(where, gpre, upre, w_gate, w_up, n, after=()):
    tokens, width = gpre.shape
    feat = w_gate.shape[0]
    tile = min(512, feat)
    sub = tokens // (2 * n)
    return pl.pallas_call(
        functools.partial(hidden_kernel, n),
        out_shape=(
            jax.ShapeDtypeStruct((n, sub, feat), bf16),
            jax.ShapeDtypeStruct((n, sub, feat), f32),
        ),
        grid_spec=pltpu.PrefetchScalarGridSpec(
            num_scalar_prefetch=1,
            grid=(feat // tile,),
            in_specs=[
                pl.BlockSpec((tokens, width), lambda i, w: (0, 0)),
                pl.BlockSpec((tokens, width), lambda i, w: (0, 0)),
                pl.BlockSpec((tile, width), lambda i, w: (i, 0)),
                pl.BlockSpec((tile, width), lambda i, w: (i, 0)),
            ]
            + [ANY] * len(after),
            out_specs=(
                pl.BlockSpec((n, sub, tile), lambda i, w: (0, 0, i)),
                pl.BlockSpec((n, sub, tile), lambda i, w: (0, 0, i)),
            ),
        ),
        compiler_params=pltpu.CompilerParams(vmem_limit_bytes=48 * 1024 * 1024),
        cost_estimate=pl.CostEstimate(
            flops=4 * tokens * width * feat,
            bytes_accessed=4 * width * (tokens + feat) + 6 * n * sub * feat,
            transcendentals=0,
        ),
    )(where, gpre, upre, w_gate, w_up, *after)


def per_device(
    stream_in, grad_out, gate_pre, up_pre, keep_mask, segment_ids, norm_gain, w_gate, w_up, w_down
):
    n_row = lax.axis_size("row")
    n_col = lax.axis_size("col")
    nz = n_col // 2
    tok_col, feat = stream_in.shape
    tok_row, width = gate_pre.shape
    total = tok_col * n_col
    sub = tok_col // CHUNKS
    col, row = lax.axis_index("col"), lax.axis_index("row")
    core, chip = lax.rem(col, 2), lax.div(col, 2)
    ring = [0] + list(range(1, nz, 2)) + list(range(nz - 2 + nz % 2, 0, -2))
    after_of = {ring[i]: ring[(i + 1) % nz] for i in range(nz)}

    def spots(chips):
        return jnp.stack([core] + [lax.bitwise_xor(c, row) for c in chips]).astype(jnp.int32)

    direct = spots([lax.bitwise_xor(chip, s) for s in range(nz)])
    held = [sum(jnp.where(chip == ring[p], ring[(p - s) % nz], 0) for p in range(nz)) for s in range(nz)]
    around = spots(held)

    def swap(a):
        return lax.ppermute(a, "col", [(i, i ^ 1) for i in range(n_col)])

    def z_step(a, s):
        return lax.ppermute(a, "col", [(i, i ^ (2 * s)) for i in range(n_col)])

    def z_next(a):
        return lax.ppermute(a, "col", [(i, 2 * after_of[i // 2] + i % 2) for i in range(n_col)])

    def row_step(a, j):
        return lax.ppermute(a, "row", [(i, i ^ j) for i in range(n_row)])

    def row_near(a):
        got = {0: a, 1: row_step(a, 1)}
        for k in range(2, n_row, 2):
            got[k] = row_step(a, k)
        return got

    def row_far(got):
        halves = {j: (got[j][0], got[j][1]) for j in got}
        for k in range(2, n_row, 2):
            halves[k + 1] = (row_step(got[1][0], k), row_step(got[k][1], 1))
        return [[halves[j][h] for j in range(n_row)] for h in range(2)]

    def row_total(a):
        got = a
        for j in range(1, n_row):
            got = got + row_step(a, j)
        return got

    def cot_part(k):
        a = grad_out[k * sub : (k + 1) * sub]
        mine = join([a] + [z_step(a, s) for s in range(1, nz)])
        return mine, swap(mine)

    xs = stream_in.astype(f32)
    onehot = (segment_ids[:, None] == jnp.arange(SEGS, dtype=jnp.int32)[None, :]).astype(f32)
    sums = row_total(jnp.concatenate([jnp.sum(xs * xs, axis=1), jnp.sum(onehot, axis=0)]))
    squares, counts = sums[:tok_col], sums[tok_col:]
    weights = jnp.sum(onehot * (total / (SEGS * counts))[None, :], axis=1)
    weights = weights.reshape(2, CHUNKS, sub, 1)
    recip = lax.rsqrt(squares / D + eps)
    normed = (xs * recip[:, None] * norm_gain[None, :]).astype(bf16)

    gate, up, keep = (a.reshape(2, CHUNKS, sub, width) for a in (gate_pre, up_pre, keep_mask))
    drop_near = row_near(masked(gate, up, keep, weights))

    cots, partials = [], []
    for k in range(CHUNKS):
        mine, other = cot_part(k)
        late = [drop_near[j] for j in drop_near if j] if k == CHUNKS - 1 else []
        cot, partial = back(direct, mine, other, w_down, late)
        cots.append(cot)
        partials.append(partial)
    drop_far = row_far(drop_near)
    dropped_full = jnp.concatenate([s for half in drop_far for s in half], axis=0)

    norm_slots = [normed]
    for s in range(1, nz):
        norm_slots.append(z_next(norm_slots[-1]))

    gathered = []
    for k in range(CHUNKS):
        parts = [row_step(partials[k][j], j) for j in range(1, n_row)]
        late = []
        if k == CHUNKS - 1:
            late = [drop_far[h][j] for h in range(2) for j in range(3, n_row, 2)] + [norm_slots[1]]
        near = row_near(hidden_grads(k, partials[k], parts, gate, up, keep, weights, late))
        gathered.append(near)

    cot_full = jnp.concatenate([c.reshape(-1, feat) for c in cots], axis=0)
    grad_down = over_tokens(dropped_full, cot_full).astype(bf16)

    normed_mine = join(norm_slots)
    normed_full = place(around, normed_mine, swap(normed_mine))
    gathered = [[jnp.concatenate(s, axis=0) for s in row_far(near)] for near in gathered]

    scaled = []
    for k in range(CHUNKS):
        late = [grad_down] + norm_slots[2:] if k == 0 else [normed_full]
        give, rest = hidden(direct, gathered[k][0], gathered[k][1], w_gate, w_up, nz, late)
        pair = (rest + swap(give).astype(f32)).astype(bf16)
        grad_normed = pair[0].astype(f32)
        for s in range(1, nz):
            grad_normed = grad_normed + z_step(pair[s], s).astype(f32)
        scaled.append(grad_normed * norm_gain[None, :])

    normed_full = normed_full.reshape(nz, 2, CHUNKS, sub, feat).transpose(2, 0, 1, 3, 4)
    normed_full = normed_full.reshape(total, feat)
    grad_gate = over_tokens(
        normed_full, jnp.concatenate([g[0] for g in gathered], axis=0)
    ).astype(bf16)
    grad_up = over_tokens(normed_full, jnp.concatenate([g[1] for g in gathered], axis=0)).astype(bf16)

    scaled = jnp.concatenate(scaled, axis=0)
    inner = row_total(jnp.sum(scaled * xs, axis=1)) / D
    branch = recip[:, None] * (scaled - xs * (recip * recip * inner)[:, None])
    grad_in = (grad_out.astype(f32) + branch).astype(bf16)
    return (grad_in, grad_gate, grad_up, grad_down)


def solution(mesh):
    return jax.shard_map(
        per_device,
        mesh=mesh,
        in_specs=(
            P("col", "row"),
            P("col", "row"),
            P("row", "col"),
            P("row", "col"),
            P("row", "col"),
            P("row"),
            P("row"),
            P("row", "col"),
            P("row", "col"),
            P("col", "row"),
        ),
        out_specs=(P("col", "row"), P("row", "col"), P("row", "col"), P("col", "row")),
        check_vma=False,
    )
```

```python
import functools

import jax
import jax.numpy as jnp
from jax import lax
from jax.experimental import pallas as pl
from jax.experimental.pallas import tpu as pltpu
from jax.sharding import PartitionSpec as P

D = 8192
SEGS = 16
LANES = 128
VMEM = 60 * 1024 * 1024
CHUNKS = 2
SHARE = 8

eps = 1e-05
keep_scale = 1.0 / 0.9
bf16 = jnp.bfloat16
f32 = jnp.float32
ANY = pl.BlockSpec(memory_space=pl.ANY)


def cost(flops, bytes_accessed, transcendentals):
    return pl.CostEstimate(
        flops=flops // SHARE,
        bytes_accessed=bytes_accessed // SHARE,
        transcendentals=transcendentals // SHARE,
    )


def over_tokens(left, right):
    return lax.dot_general(left, right, (((0,), (0,)), ((), ())), preferred_element_type=f32)


def over_width(left, right):
    return lax.dot_general(left, right, (((1,), (1,)), ((), ())), preferred_element_type=f32)


def join_kernel(n, *refs):
    parts, out, sems = refs[:n], refs[-2], refs[-1]
    copies = [pltpu.make_async_copy(parts[s], out.at[s], sems.at[s]) for s in range(n)]
    for copy in copies:
        copy.start()
    for copy in copies:
        copy.wait()


def join(parts, after=()):
    n = len(parts)
    shape = (n,) + parts[0].shape
    return pl.pallas_call(
        functools.partial(join_kernel, n),
        out_shape=jax.ShapeDtypeStruct(shape, parts[0].dtype),
        in_specs=[ANY] * (n + len(after)),
        scratch_shapes=[pltpu.SemaphoreType.DMA((n,))],
        compiler_params=pltpu.CompilerParams(vmem_limit_bytes=VMEM),
        cost_estimate=cost(
            flops=0, bytes_accessed=4 * n * parts[0].size, transcendentals=0
        ),
    )(*parts, *after)


def fill(n, where, mine, other, out, sems):
    core = where[0]
    copies = []
    for s in range(n):
        copies.append(pltpu.make_async_copy(mine.at[s], out.at[where[1 + s], core], sems.at[s]))
        copies.append(
            pltpu.make_async_copy(other.at[s], out.at[where[1 + s], 1 - core], sems.at[n + s])
        )
    for copy in copies:
        copy.start()
    for copy in copies:
        copy.wait()


def gather_slots(plan, refs, out, sems, first):
    copies = []
    for at, (ref, half) in enumerate(plan):
        source = refs[ref] if half is None else refs[ref].at[half]
        copies.append(pltpu.make_async_copy(source, out.at[at], sems.at[first + at]))
    return copies


def take_kernel(n, a_ref, *refs):
    for s in range(n):
        refs[-1][s] = a_ref[...]


def take(a, k, sub, n, after=()):
    feat = a.shape[1]
    return pl.pallas_call(
        functools.partial(take_kernel, n),
        out_shape=jax.ShapeDtypeStruct((n, sub, feat), a.dtype),
        grid=(1,),
        in_specs=[pl.BlockSpec((sub, feat), lambda i: (k, 0))] + [ANY] * len(after),
        out_specs=pl.BlockSpec((n, sub, feat), lambda i: (0, 0, 0)),
        compiler_params=pltpu.CompilerParams(vmem_limit_bytes=VMEM),
        cost_estimate=cost(flops=0, bytes_accessed=2 * (n + 1) * sub * feat, transcendentals=0),
    )(a, *after)


def pick_kernel(a_ref, *refs):
    refs[-1][...] = a_ref[...]


def pick(a, h, after=()):
    shape = a.shape[1:]
    return pl.pallas_call(
        pick_kernel,
        out_shape=jax.ShapeDtypeStruct(shape, a.dtype),
        grid=(1,),
        in_specs=[pl.BlockSpec((None,) + shape, lambda i: (h, 0, 0))] + [ANY] * len(after),
        out_specs=pl.BlockSpec(shape, lambda i: (0, 0)),
        compiler_params=pltpu.CompilerParams(vmem_limit_bytes=VMEM),
        cost_estimate=cost(flops=0, bytes_accessed=2 * a.size, transcendentals=0),
    )(a, *after)


def hold_kernel(a_ref, *refs):
    refs[-1][...] = a_ref[...]


def hold(a, after):
    whole = pl.BlockSpec(a.shape, lambda i: (0, 0, 0))
    return pl.pallas_call(
        hold_kernel,
        out_shape=jax.ShapeDtypeStruct(a.shape, a.dtype),
        grid=(1,),
        in_specs=[whole] + [ANY] * len(after),
        out_specs=whole,
        compiler_params=pltpu.CompilerParams(vmem_limit_bytes=VMEM),
        cost_estimate=cost(flops=0, bytes_accessed=4 * a.size, transcendentals=0),
    )(a, *after)


def normed_kernel(n, x_ref, recip_ref, gain_ref, *refs):
    normed = (x_ref[...].astype(f32) * recip_ref[...] * gain_ref[...]).astype(bf16)
    for s in range(n):
        refs[-1][s] = normed


def normalize(x, recip, gain, n, after=()):
    return pl.pallas_call(
        functools.partial(normed_kernel, n),
        out_shape=jax.ShapeDtypeStruct((n,) + x.shape, bf16),
        grid=(1,),
        in_specs=[pl.BlockSpec(a.shape, lambda i: (0, 0)) for a in (x, recip, gain)]
        + [ANY] * len(after),
        out_specs=pl.BlockSpec((n,) + x.shape, lambda i: (0, 0, 0)),
        compiler_params=pltpu.CompilerParams(vmem_limit_bytes=VMEM),
        cost_estimate=cost(
            flops=2 * x.size, bytes_accessed=2 * (n + 1) * x.size, transcendentals=0
        ),
    )(x, recip, gain, *after)


def pair_kernel(rest_ref, got_ref, *refs):
    refs[-1][...] = (rest_ref[...] + got_ref[...].astype(f32)).astype(bf16)


def add_pair(rest, got, after=()):
    whole = pl.BlockSpec(rest.shape, lambda i: (0, 0, 0))
    return pl.pallas_call(
        pair_kernel,
        out_shape=jax.ShapeDtypeStruct(rest.shape, bf16),
        grid=(1,),
        in_specs=[whole, whole] + [ANY] * len(after),
        out_specs=whole,
        compiler_params=pltpu.CompilerParams(vmem_limit_bytes=VMEM),
        cost_estimate=cost(flops=rest.size, bytes_accessed=8 * rest.size, transcendentals=0),
    )(rest, got, *after)


def settle_kernel(parts, gain, x, *refs):
    scaled_ref, inner_ref = refs[-2:]
    total = jnp.sum(parts[...].astype(f32), axis=0)
    scaled = total * gain[...]
    scaled_ref[...] = scaled
    inner = jnp.sum(scaled * x[...].astype(f32), axis=1, keepdims=True)
    inner_ref[...] = jnp.broadcast_to(inner, inner_ref.shape)


def settle(k, parts, gain, x, after=()):
    n, sub, feat = parts.shape
    block = pl.BlockSpec((sub, feat), lambda i: (0, 0))
    return pl.pallas_call(
        settle_kernel,
        out_shape=(
            jax.ShapeDtypeStruct((sub, feat), f32),
            jax.ShapeDtypeStruct((sub, LANES), f32),
        ),
        grid=(1,),
        in_specs=[
            pl.BlockSpec((n, sub, feat), lambda i: (0, 0, 0)),
            pl.BlockSpec((1, feat), lambda i: (0, 0)),
            pl.BlockSpec((sub, feat), lambda i: (k, 0)),
        ]
        + [ANY] * len(after),
        out_specs=(block, pl.BlockSpec((sub, LANES), lambda i: (0, 0))),
        compiler_params=pltpu.CompilerParams(vmem_limit_bytes=VMEM),
        cost_estimate=cost(
            flops=6 * sub * feat, bytes_accessed=14 * sub * feat, transcendentals=0
        ),
    )(parts, gain, x, *after)


def weight_grads_kernel(n, plan, count, where, mine, other, *refs):
    rights = refs[:count]
    left, right, sems = refs[-3:]
    gate_ref, up_ref = refs[-5:-3]
    sub = left.shape[3]
    step, tile = pl.program_id(0), gate_ref.shape[0]

    @pl.when(step == 0)
    def _():
        core = where[0]
        copies = []
        for s in range(n):
            for k in range(CHUNKS):
                rows = pl.ds(k * sub, sub)
                at = where[1 + s]
                copies.append((mine.at[s, rows], left.at[k, at, core]))
                copies.append((other.at[s, rows], left.at[k, at, 1 - core]))
        copies = [pltpu.make_async_copy(a, b, sems.at[i]) for i, (a, b) in enumerate(copies)]
        copies += gather_slots(plan, rights, right, sems, len(copies))
        for copy in copies:
            copy.start()
        for copy in copies:
            copy.wait()

    columns = pl.ds(pl.multiple_of(step * tile, tile), tile)
    a = left[:, :, :, :, columns].reshape(-1, tile)
    for q, out in enumerate((gate_ref, up_ref)):
        b = right[q * len(plan) // 2 : (q + 1) * len(plan) // 2].reshape(a.shape[0], -1)
        out[...] = over_tokens(a, b).astype(bf16)


def weight_grads(where, mine, other, slots, plan, after=()):
    n, tok, feat = mine.shape
    size, width = slots[0].shape[1:]
    tile = min(512, feat)
    tokens = 2 * n * tok
    return pl.pallas_call(
        functools.partial(weight_grads_kernel, n, plan, len(slots)),
        out_shape=(jax.ShapeDtypeStruct((feat, width), bf16),) * 2,
        grid=(feat // tile,),
        in_specs=[pl.BlockSpec(memory_space=pltpu.SMEM)] + [ANY] * (2 + len(slots) + len(after)),
        out_specs=(pl.BlockSpec((tile, width), lambda i: (i, 0)),) * 2,
        scratch_shapes=[
            pltpu.VMEM((CHUNKS, n, 2, tok // CHUNKS, feat), bf16),
            pltpu.VMEM((len(plan), size, width), bf16),
            pltpu.SemaphoreType.DMA((2 * n * CHUNKS + len(plan),)),
        ],
        compiler_params=pltpu.CompilerParams(vmem_limit_bytes=VMEM),
        cost_estimate=cost(
            flops=4 * tokens * width * feat,
            bytes_accessed=2 * (tokens * feat + 2 * tokens * width + 2 * width * feat),
            transcendentals=0,
        ),
    )(where, mine, other, *slots, *after)


def back_kernel(n, where, mine, other, w_ref, *refs):
    cot, parts, sems = refs[-n - 2], refs[-n - 1 : -1], refs[-1]
    size = 2 * cot.shape[2]

    @pl.when(pl.program_id(0) == 0)
    def _():
        fill(n, where, mine, other, cot, sems)

    left = cot[...].reshape(-1, cot.shape[-1])
    out = over_width(left, w_ref[...]).astype(bf16)
    for j in range(n):
        parts[j][:size] = out[j * size : (j + 1) * size]
        if parts[j].shape[0] > size:
            parts[j][size:] = refs[0][...]


def back(where, mine, other, w_down, more, after=()):
    n, sub, feat = mine.shape
    size = 2 * sub + sum(a.shape[0] for a in more)
    width = w_down.shape[0]
    tile = width // 2 if width // 2 % 128 == 0 else width
    tokens = 2 * n * sub
    return pl.pallas_call(
        functools.partial(back_kernel, n),
        out_shape=(
            jax.ShapeDtypeStruct((n, 2, sub, feat), bf16),
        )
        + (jax.ShapeDtypeStruct((size, width), bf16),) * n,
        grid=(width // tile,),
        in_specs=[
            pl.BlockSpec(memory_space=pltpu.SMEM),
            ANY,
            ANY,
            pl.BlockSpec((tile, feat), lambda i: (i, 0)),
        ]
        + [pl.BlockSpec((a.shape[0], tile), lambda i: (0, i)) for a in more]
        + [ANY] * len(after),
        out_specs=(
            pl.BlockSpec((n, 2, sub, feat), lambda i: (0, 0, 0, 0)),
        )
        + (pl.BlockSpec((size, tile), lambda i: (0, i)),) * n,
        scratch_shapes=[pltpu.SemaphoreType.DMA((2 * n,))],
        compiler_params=pltpu.CompilerParams(vmem_limit_bytes=VMEM),
        cost_estimate=cost(
            flops=2 * tokens * width * feat,
            bytes_accessed=2 * (2 * tokens * feat + width * feat + tokens * width),
            transcendentals=0,
        ),
    )(where, mine, other, w_down, *more, *after)


def masked_kernel(gate_ref, up_ref, keep_ref, *outs):
    for k in range(CHUNKS):
        gate = gate_ref[:, k].astype(f32)
        scale = keep_ref[:, k].astype(f32) * keep_scale
        value = gate * jax.nn.sigmoid(gate) * up_ref[:, k].astype(f32) * scale
        outs[k][...] = value.astype(bf16).reshape(outs[k].shape)


def masked(gate, up, keep):
    two, chunks, sub, width = gate.shape
    tile = width // 2 if width // 2 % 128 == 0 else width
    return pl.pallas_call(
        masked_kernel,
        out_shape=(jax.ShapeDtypeStruct((two * sub, width), bf16),) * chunks,
        grid=(width // tile,),
        in_specs=[pl.BlockSpec((two, chunks, sub, tile), lambda i: (0, 0, 0, i))] * 3,
        out_specs=(pl.BlockSpec((two * sub, tile), lambda i: (0, i)),) * chunks,
        compiler_params=pltpu.CompilerParams(vmem_limit_bytes=VMEM),
        cost_estimate=cost(
            flops=10 * gate.size, bytes_accessed=10 * gate.size, transcendentals=gate.size
        ),
    )(gate, up, keep)


def grads_kernel(n, *refs):
    parts = refs[:n]
    gate_ref, up_ref, keep_ref, weight_ref = refs[n : n + 4]
    out = refs[-1]
    total = parts[0][...].astype(f32)
    for part in parts[1:]:
        total = total + part[...].astype(f32)
    two, sub, tile = gate_ref.shape
    total = total.reshape(two, sub, tile)
    gate, up = gate_ref[...].astype(f32), up_ref[...].astype(f32)
    act = total * (keep_ref[...].astype(f32) * keep_scale * weight_ref[...])
    sig = jax.nn.sigmoid(gate)
    gpre = act * up * sig * (1.0 + gate * (1.0 - sig))
    out[0] = gpre.astype(bf16).reshape(out.shape[1:])
    out[1] = (act * gate * sig).astype(bf16).reshape(out.shape[1:])


def hidden_grads(k, parts, gate, up, keep, weights, after=()):
    n = len(parts)
    two, chunks, sub, width = gate.shape
    tile = width // 2 if width // 2 % 128 == 0 else width
    block = pl.BlockSpec((two, None, sub, tile), lambda i: (0, k, 0, i))
    size = two * sub * width
    return pl.pallas_call(
        functools.partial(grads_kernel, n),
        out_shape=jax.ShapeDtypeStruct((2, two * sub, width), bf16),
        grid=(width // tile,),
        in_specs=[pl.BlockSpec((two * sub, tile), lambda i: (0, i))] * n
        + [block] * 3
        + [pl.BlockSpec((two, None, sub, 1), lambda i: (0, k, 0, 0))]
        + [ANY] * len(after),
        out_specs=pl.BlockSpec((2, two * sub, tile), lambda i: (0, 0, i)),
        compiler_params=pltpu.CompilerParams(vmem_limit_bytes=VMEM),
        cost_estimate=cost(
            flops=20 * size, bytes_accessed=(12 + 2 * n) * size, transcendentals=size
        ),
    )(*parts, gate, up, keep, weights, *after)


def hidden_kernel(n, plan, count, where, *refs):
    slots, (wg_ref, wu_ref) = refs[:count], refs[count : count + 2]
    give_ref, keep_ref, left, sems = refs[-4:]

    @pl.when(pl.program_id(0) == 0)
    def _():
        copies = gather_slots(plan, slots, left, sems, 0)
        for copy in copies:
            copy.start()
        for copy in copies:
            copy.wait()

    half = len(plan) // 2
    width = left.shape[2]
    gpre = left[:half].reshape(-1, width)
    upre = left[half:].reshape(-1, width)
    part = over_width(gpre, wg_ref[...]) + over_width(upre, wu_ref[...])
    sub = give_ref.shape[1]
    part = part.reshape(n, 2, sub, part.shape[1])
    low = where[0] == 0
    for j in range(n):
        at = where[1 + j]
        keep_ref[at] = jnp.where(low, part[j, 0], part[j, 1])
        give_ref[at] = jnp.where(low, part[j, 1], part[j, 0]).astype(bf16)


def hidden(where, slots, plan, w_gate, w_up, n, after=()):
    size, width = slots[0].shape[1:]
    feat = w_gate.shape[0]
    tile = min(512, feat)
    tokens = len(plan) // 2 * size
    sub = tokens // (2 * n)
    return pl.pallas_call(
        functools.partial(hidden_kernel, n, plan, len(slots)),
        out_shape=(
            jax.ShapeDtypeStruct((n, sub, feat), bf16),
            jax.ShapeDtypeStruct((n, sub, feat), f32),
        ),
        grid=(feat // tile,),
        in_specs=[pl.BlockSpec(memory_space=pltpu.SMEM)]
        + [ANY] * len(slots)
        + [pl.BlockSpec((tile, width), lambda i: (i, 0))] * 2
        + [ANY] * len(after),
        out_specs=(pl.BlockSpec((n, sub, tile), lambda i: (0, 0, i)),) * 2,
        scratch_shapes=[
            pltpu.VMEM((len(plan), size, width), bf16),
            pltpu.SemaphoreType.DMA((len(plan),)),
        ],
        compiler_params=pltpu.CompilerParams(vmem_limit_bytes=VMEM),
        cost_estimate=cost(
            flops=4 * tokens * width * feat,
            bytes_accessed=4 * width * (tokens + feat) + 6 * n * sub * feat,
            transcendentals=0,
        ),
    )(where, *slots, w_gate, w_up, *after)


def down_grad_kernel(plan, count, weight_ref, *refs):
    drops, cots = refs[:count], refs[count : count + CHUNKS]
    out, left, right, sems = refs[-4:]
    step, tile = pl.program_id(0), out.shape[0]

    @pl.when(step == 0)
    def _():
        copies = gather_slots(plan, drops, left, sems, 0)
        for k in range(CHUNKS):
            copies.append(pltpu.make_async_copy(cots[k], right.at[k], sems.at[len(plan) + k]))
        for copy in copies:
            copy.start()
        for copy in copies:
            copy.wait()

    columns = pl.ds(pl.multiple_of(step * tile, tile), tile)
    a = left[:, :, columns].astype(f32) * weight_ref[...]
    a = a.astype(bf16).reshape(-1, tile)
    out[...] = over_tokens(a, right[...].reshape(a.shape[0], -1)).astype(bf16)


def down_grad(weights, drops, plan, cots, after=()):
    size, width = drops[0].shape
    feat = cots[0].shape[-1]
    tile = 256 if width % 256 == 0 else 128
    tokens = len(plan) * size
    return pl.pallas_call(
        functools.partial(down_grad_kernel, plan, len(drops)),
        out_shape=jax.ShapeDtypeStruct((width, feat), bf16),
        grid=(width // tile,),
        in_specs=[pl.BlockSpec((len(plan), size, 1), lambda i: (0, 0, 0))]
        + [ANY] * (len(drops) + len(cots) + len(after)),
        out_specs=pl.BlockSpec((tile, feat), lambda i: (i, 0)),
        scratch_shapes=[
            pltpu.VMEM((len(plan), size, width), bf16),
            pltpu.VMEM((CHUNKS,) + cots[0].shape, bf16),
            pltpu.SemaphoreType.DMA((len(plan) + CHUNKS,)),
        ],
        compiler_params=pltpu.CompilerParams(vmem_limit_bytes=VMEM),
        cost_estimate=cost(
            flops=2 * tokens * width * feat,
            bytes_accessed=2 * (tokens * feat + tokens * width + width * feat),
            transcendentals=0,
        ),
    )(weights, *drops, *cots, *after)


def per_device(
    stream_in, grad_out, gate_pre, up_pre, keep_mask, segment_ids, norm_gain, w_gate, w_up, w_down
):
    n_row = lax.axis_size("row")
    n_col = lax.axis_size("col")
    nz = n_col // 2
    tok_col, feat = stream_in.shape
    tok_row, width = gate_pre.shape
    total = tok_col * n_col
    sub = tok_col // CHUNKS
    col, row = lax.axis_index("col"), lax.axis_index("row")
    core, chip = lax.rem(col, 2), lax.div(col, 2)
    ring = [0] + list(range(1, nz, 2)) + list(range(nz - 2 + nz % 2, 0, -2))
    after_of = {ring[i]: ring[(i + 1) % nz] for i in range(nz)}

    def spots(chips):
        return jnp.stack([core] + [lax.bitwise_xor(c, row) for c in chips]).astype(jnp.int32)

    held = [sum(jnp.where(chip == ring[p], ring[(p - s) % nz], 0) for p in range(nz)) for s in range(nz)]
    around = spots(held)
    along = spots(range(nz))
    z_groups = [[2 * z + c for z in range(nz)] for c in range(2)]

    def swap(a):
        return lax.ppermute(a, "col", [(i, i ^ 1) for i in range(n_col)])

    def z_exchange(a):
        return lax.all_to_all(
            a, "col", split_axis=0, concat_axis=0, axis_index_groups=z_groups, tiled=True
        )

    def z_next(a):
        return lax.ppermute(a, "col", [(i, 2 * after_of[i // 2] + i % 2) for i in range(n_col)])

    def row_step(a, j):
        return lax.ppermute(a, "row", [(i, i ^ j) for i in range(n_row)])

    def near(a):
        return {j: row_step(a, j) for j in [1] + list(range(2, n_row, 2))}

    def far(got):
        return {k + 1: (row_step(a, k), row_step(b, 1)) for k, (a, b) in got.items()}

    def to_pass(got, after=()):
        first = pick(got[1], 0, after)
        return {k: (first, pick(got[k], 1, after)) for k in range(2, n_row, 2)}

    def all_slots(own, near_ones, far_ones):
        return [own] + list(near_ones.values()) + [a for two in far_ones.values() for a in two]

    nears, fars = [0, 1] + list(range(2, n_row, 2)), list(range(3, n_row, 2))

    def plan_of(half, base=0):
        return [
            (base + nears.index(j), half)
            if j in nears
            else (base + len(nears) + 2 * fars.index(j) + half, None)
            for j in range(n_row)
        ]

    def row_total(a):
        j = 1
        while j < n_row:
            a = a + row_step(a, j)
            j = 2 * j
        return a

    gate, up, keep = (a.reshape(2, CHUNKS, sub, width) for a in (gate_pre, up_pre, keep_mask))
    drop = masked(gate, up, keep)
    assert CHUNKS == 2
    drop_near = [near(a) for a in drop]
    drop_far = far({k: (drop_near[0][1], drop_near[1][k]) for k in range(2, n_row, 2)})
    drop_slots = [
        [drop[h]]
        + [drop_near[h][j] if j in drop_near[h] else drop_far[j][h] for j in range(1, n_row)]
        for h in range(CHUNKS)
    ]
    drops = drop_slots[0] + drop_slots[1]
    far_ones = [a for two in drop_far.values() for a in two]

    xs = stream_in.astype(f32)
    left_over = jnp.sum(xs * xs, axis=1)
    rows = [segment_ids.astype(f32)]
    for _ in range(3):
        rows.append(lax.reduce_precision(left_over, 8, 7))
        left_over = left_over - rows[-1]
    note = jnp.stack([jnp.pad(a, (0, width - a.shape[0])) for a in rows]).astype(bf16)
    note = jnp.pad(note, ((0, 12), (0, 0)))
    gain = norm_gain.reshape(1, feat)

    def read(notes):
        notes = jnp.stack([a[:4].astype(f32) for a in notes])
        onehot = (notes[:, 0, :tok_row, None] == jnp.arange(SEGS, dtype=f32)).astype(f32)
        counts = jnp.sum(onehot, axis=(0, 1))
        weights = jnp.sum(onehot * (total / (SEGS * counts)), axis=2)
        squares = jnp.sum(notes[:, 3, :tok_col] + notes[:, 2, :tok_col] + notes[:, 1, :tok_col], axis=0)
        recip = lax.rsqrt(squares / D + eps)
        return weights.reshape(n_row, 2, CHUNKS, sub), recip[:, None]

    def cot_gather(k, after):
        if k == 0:
            slots = [take(grad_out, 0, sub, 1, [drop[0]])[0]]
            for s in range(1, nz):
                slots.append(z_next(slots[-1]))
            return around, join(
                slots, [a for got in drop_near + [dict(enumerate(far_ones))] for a in got.values()]
            )
        return along, z_exchange(take(grad_out, k, sub, nz, after))

    cots, hids, hid_near, pairs, settled, slots = [], [], [], [], [], []
    plans = [[], []]
    plan = plan_of(0) + plan_of(1)

    def multiply(k, passed, after):
        mine = all_slots(hids[k], hid_near[k], far(passed))
        give, rest = hidden(along, mine, plan, w_gate, w_up, nz, after)
        for h in range(2):
            plans[h].extend(plan_of(h, len(slots)))
        slots.extend(mine)
        pairs.append(add_pair(rest, swap(give)))
        return give

    for k in range(CHUNKS):
        if k == 0:
            where, mine = cot_gather(0, [])
            other = swap(mine)
            late = []
        else:
            where, mine = along, z_exchange(take(grad_out, k, sub, nz, [other]))
            mine = hold(mine, [hids[-1]])
            other = swap(mine)
            late = [normed] if k == 1 else []
        cot, *partial = back(where, mine, other, w_down, [] if k else [note], late)
        cots.append(cot)
        parts = [partial[0]] + [row_step(partial[j], j) for j in range(1, n_row)]
        if k == 0:
            every, recip = read([a[2 * sub :] for a in parts])
            weights = every[0][:, :, :, None]
            all_weights = every.transpose(2, 0, 1, 3).reshape(CHUNKS * n_row, 2 * sub, 1)
            late = []
        else:
            late = [multiply(k - 1, to_pass(hid_near[-1], [partial[0]]), pairs[-1:])]
        hids.append(hidden_grads(k, parts, gate, up, keep, weights, late))
        hid_near.append(near(hids[k]))
        if k == 0:
            normed = normalize(stream_in, recip, gain, nz, [hids[0]])
            normed_mine = z_exchange(normed)
    order = [(i, None) for i in range(len(drops))]
    grad_down = down_grad(all_weights, drops, order, cots, [hids[-1]])
    multiply(CHUNKS - 1, to_pass(hid_near[-1], [grad_down]), pairs[-1:])
    normed_other = swap(normed_mine)
    for k in range(CHUNKS):
        late = []
        if k == CHUNKS - 1:
            grad_gate, grad_up = weight_grads(
                along,
                normed_mine,
                normed_other,
                slots,
                plans[0] + plans[1],
                pairs[-1:] + [s[1] for s in settled],
            )
            late = [grad_gate]
        settled.append(settle(k, z_exchange(pairs[k]), gain, stream_in, late))
    scaled = jnp.concatenate([s[0] for s in settled], axis=0)
    inner = jnp.concatenate([s[1] for s in settled], axis=0)
    inner = inner + sum(row_step(inner, j) for j in range(1, n_row))
    inner = inner[:, :1] / D
    branch = recip * (scaled - xs * (recip * recip * inner))
    grad_in = (grad_out.astype(f32) + branch).astype(bf16)
    return (grad_in, grad_gate, grad_up, grad_down)


def solution(mesh):
    return jax.shard_map(
        per_device,
        mesh=mesh,
        in_specs=(
            P("col", "row"),
            P("col", "row"),
            P("row", "col"),
            P("row", "col"),
            P("row", "col"),
            P("row"),
            P("row"),
            P("row", "col"),
            P("row", "col"),
            P("col", "row"),
        ),
        out_specs=(P("col", "row"), P("row", "col"), P("row", "col"), P("col", "row")),
        check_vma=False,
    )
```

```python
import functools

import jax
import jax.numpy as jnp
from jax import lax
from jax.experimental import pallas as pl
from jax.experimental.pallas import tpu as pltpu
from jax.sharding import PartitionSpec as P

D = 8192
SEGS = 16
LANES = 128
VMEM = 60 * 1024 * 1024
CHUNKS = 2
SHARE = 8

eps = 1e-05
keep_scale = 1.0 / 0.9
bf16 = jnp.bfloat16
f32 = jnp.float32
ANY = pl.BlockSpec(memory_space=pl.ANY)


def cost(flops, bytes_accessed, transcendentals):
    return pl.CostEstimate(
        flops=flops // SHARE,
        bytes_accessed=bytes_accessed // SHARE,
        transcendentals=transcendentals // SHARE,
    )


def over_tokens(left, right):
    return lax.dot_general(left, right, (((0,), (0,)), ((), ())), preferred_element_type=f32)


def over_width(left, right):
    return lax.dot_general(left, right, (((1,), (1,)), ((), ())), preferred_element_type=f32)


def join_kernel(n, *refs):
    parts, out, sems = refs[:n], refs[-2], refs[-1]
    copies = [pltpu.make_async_copy(parts[s], out.at[s], sems.at[s]) for s in range(n)]
    for copy in copies:
        copy.start()
    for copy in copies:
        copy.wait()


def join(parts, after=()):
    n = len(parts)
    shape = (n,) + parts[0].shape
    return pl.pallas_call(
        functools.partial(join_kernel, n),
        out_shape=jax.ShapeDtypeStruct(shape, parts[0].dtype),
        in_specs=[ANY] * (n + len(after)),
        scratch_shapes=[pltpu.SemaphoreType.DMA((n,))],
        compiler_params=pltpu.CompilerParams(vmem_limit_bytes=VMEM),
        cost_estimate=cost(
            flops=0, bytes_accessed=4 * n * parts[0].size, transcendentals=0
        ),
    )(*parts, *after)


def fill(n, where, mine, other, out, sems):
    core = where[0]
    copies = []
    for s in range(n):
        copies.append(pltpu.make_async_copy(mine.at[s], out.at[where[1 + s], core], sems.at[s]))
        copies.append(
            pltpu.make_async_copy(other.at[s], out.at[where[1 + s], 1 - core], sems.at[n + s])
        )
    for copy in copies:
        copy.start()
    for copy in copies:
        copy.wait()


def gather_slots(plan, refs, out, sems, first):
    copies = []
    for at, (ref, half) in enumerate(plan):
        source = refs[ref] if half is None else refs[ref].at[half]
        copies.append(pltpu.make_async_copy(source, out.at[at], sems.at[first + at]))
    return copies


def take_kernel(n, a_ref, *refs):
    for s in range(n):
        refs[-1][s] = a_ref[...]


def take(a, k, sub, n, after=()):
    feat = a.shape[1]
    return pl.pallas_call(
        functools.partial(take_kernel, n),
        out_shape=jax.ShapeDtypeStruct((n, sub, feat), a.dtype),
        grid=(1,),
        in_specs=[pl.BlockSpec((sub, feat), lambda i: (k, 0))] + [ANY] * len(after),
        out_specs=pl.BlockSpec((n, sub, feat), lambda i: (0, 0, 0)),
        compiler_params=pltpu.CompilerParams(vmem_limit_bytes=VMEM),
        cost_estimate=cost(flops=0, bytes_accessed=2 * (n + 1) * sub * feat, transcendentals=0),
    )(a, *after)


def pick_kernel(a_ref, *refs):
    refs[-1][...] = a_ref[...]


def pick(a, h, after=()):
    shape = a.shape[1:]
    return pl.pallas_call(
        pick_kernel,
        out_shape=jax.ShapeDtypeStruct(shape, a.dtype),
        grid=(1,),
        in_specs=[pl.BlockSpec((None,) + shape, lambda i: (h, 0, 0))] + [ANY] * len(after),
        out_specs=pl.BlockSpec(shape, lambda i: (0, 0)),
        compiler_params=pltpu.CompilerParams(vmem_limit_bytes=VMEM),
        cost_estimate=cost(flops=0, bytes_accessed=2 * a.size, transcendentals=0),
    )(a, *after)


def hold_kernel(a_ref, *refs):
    refs[-1][...] = a_ref[...]


def hold(a, after):
    whole = pl.BlockSpec(a.shape, lambda i: (0, 0, 0))
    return pl.pallas_call(
        hold_kernel,
        out_shape=jax.ShapeDtypeStruct(a.shape, a.dtype),
        grid=(1,),
        in_specs=[whole] + [ANY] * len(after),
        out_specs=whole,
        compiler_params=pltpu.CompilerParams(vmem_limit_bytes=VMEM),
        cost_estimate=cost(flops=0, bytes_accessed=4 * a.size, transcendentals=0),
    )(a, *after)


def normed_kernel(n, x_ref, recip_ref, gain_ref, *refs):
    normed = (x_ref[...].astype(f32) * recip_ref[...] * gain_ref[...]).astype(bf16)
    for s in range(n):
        refs[-1][s] = normed


def normalize(x, recip, gain, n, after=()):
    return pl.pallas_call(
        functools.partial(normed_kernel, n),
        out_shape=jax.ShapeDtypeStruct((n,) + x.shape, bf16),
        grid=(1,),
        in_specs=[pl.BlockSpec(a.shape, lambda i: (0, 0)) for a in (x, recip, gain)]
        + [ANY] * len(after),
        out_specs=pl.BlockSpec((n,) + x.shape, lambda i: (0, 0, 0)),
        compiler_params=pltpu.CompilerParams(vmem_limit_bytes=VMEM),
        cost_estimate=cost(
            flops=2 * x.size, bytes_accessed=2 * (n + 1) * x.size, transcendentals=0
        ),
    )(x, recip, gain, *after)


def pair_kernel(rest_ref, got_ref, *refs):
    refs[-1][...] = (rest_ref[...] + got_ref[...].astype(f32)).astype(bf16)


def add_pair(rest, got, after=()):
    whole = pl.BlockSpec(rest.shape, lambda i: (0, 0, 0))
    return pl.pallas_call(
        pair_kernel,
        out_shape=jax.ShapeDtypeStruct(rest.shape, bf16),
        grid=(1,),
        in_specs=[whole, whole] + [ANY] * len(after),
        out_specs=whole,
        compiler_params=pltpu.CompilerParams(vmem_limit_bytes=VMEM),
        cost_estimate=cost(flops=rest.size, bytes_accessed=8 * rest.size, transcendentals=0),
    )(rest, got, *after)


def settle_kernel(parts, gain, x, *refs):
    scaled_ref, inner_ref = refs[-2:]
    total = jnp.sum(parts[...].astype(f32), axis=0)
    scaled = total * gain[...]
    scaled_ref[...] = scaled
    inner = jnp.sum(scaled * x[...].astype(f32), axis=1, keepdims=True)
    inner_ref[...] = jnp.broadcast_to(inner, inner_ref.shape)


def settle(k, parts, gain, x, after=()):
    n, sub, feat = parts.shape
    block = pl.BlockSpec((sub, feat), lambda i: (0, 0))
    return pl.pallas_call(
        settle_kernel,
        out_shape=(
            jax.ShapeDtypeStruct((sub, feat), f32),
            jax.ShapeDtypeStruct((sub, LANES), f32),
        ),
        grid=(1,),
        in_specs=[
            pl.BlockSpec((n, sub, feat), lambda i: (0, 0, 0)),
            pl.BlockSpec((1, feat), lambda i: (0, 0)),
            pl.BlockSpec((sub, feat), lambda i: (k, 0)),
        ]
        + [ANY] * len(after),
        out_specs=(block, pl.BlockSpec((sub, LANES), lambda i: (0, 0))),
        compiler_params=pltpu.CompilerParams(vmem_limit_bytes=VMEM),
        cost_estimate=cost(
            flops=6 * sub * feat, bytes_accessed=14 * sub * feat, transcendentals=0
        ),
    )(parts, gain, x, *after)


def weight_grads_kernel(n, plan, count, where, mine, other, *refs):
    rights = refs[:count]
    left, right, sems = refs[-3:]
    gate_ref, up_ref = refs[-5:-3]
    sub = left.shape[3]
    step, tile = pl.program_id(0), gate_ref.shape[0]

    @pl.when(step == 0)
    def _():
        core = where[0]
        copies = []
        for s in range(n):
            for k in range(CHUNKS):
                rows = pl.ds(k * sub, sub)
                at = where[1 + s]
                copies.append((mine.at[s, rows], left.at[k, at, core]))
                copies.append((other.at[s, rows], left.at[k, at, 1 - core]))
        copies = [pltpu.make_async_copy(a, b, sems.at[i]) for i, (a, b) in enumerate(copies)]
        copies += gather_slots(plan, rights, right, sems, len(copies))
        for copy in copies:
            copy.start()
        for copy in copies:
            copy.wait()

    columns = pl.ds(pl.multiple_of(step * tile, tile), tile)
    a = left[:, :, :, :, columns].reshape(-1, tile)
    for q, out in enumerate((gate_ref, up_ref)):
        b = right[q * len(plan) // 2 : (q + 1) * len(plan) // 2].reshape(a.shape[0], -1)
        out[...] = over_tokens(a, b).astype(bf16)


def weight_grads(where, mine, other, slots, plan, after=()):
    n, tok, feat = mine.shape
    size, width = slots[0].shape[1:]
    tile = min(512, feat)
    tokens = 2 * n * tok
    return pl.pallas_call(
        functools.partial(weight_grads_kernel, n, plan, len(slots)),
        out_shape=(jax.ShapeDtypeStruct((feat, width), bf16),) * 2,
        grid=(feat // tile,),
        in_specs=[pl.BlockSpec(memory_space=pltpu.SMEM)] + [ANY] * (2 + len(slots) + len(after)),
        out_specs=(pl.BlockSpec((tile, width), lambda i: (i, 0)),) * 2,
        scratch_shapes=[
            pltpu.VMEM((CHUNKS, n, 2, tok // CHUNKS, feat), bf16),
            pltpu.VMEM((len(plan), size, width), bf16),
            pltpu.SemaphoreType.DMA((2 * n * CHUNKS + len(plan),)),
        ],
        compiler_params=pltpu.CompilerParams(vmem_limit_bytes=VMEM),
        cost_estimate=cost(
            flops=4 * tokens * width * feat,
            bytes_accessed=2 * (tokens * feat + 2 * tokens * width + 2 * width * feat),
            transcendentals=0,
        ),
    )(where, mine, other, *slots, *after)


def back_kernel(n, where, mine, other, w_ref, *refs):
    cot, parts, sems = refs[-n - 2], refs[-n - 1 : -1], refs[-1]
    size = 2 * cot.shape[2]

    @pl.when(pl.program_id(0) == 0)
    def _():
        fill(n, where, mine, other, cot, sems)

    left = cot[...].reshape(-1, cot.shape[-1])
    out = over_width(left, w_ref[...]).astype(bf16)
    for j in range(n):
        parts[j][:size] = out[j * size : (j + 1) * size]
        if parts[j].shape[0] > size:
            parts[j][size:] = refs[0][...]


def back(where, mine, other, w_down, more, after=()):
    n, sub, feat = mine.shape
    size = 2 * sub + sum(a.shape[0] for a in more)
    width = w_down.shape[0]
    tile = width // 2 if width // 2 % 128 == 0 else width
    tokens = 2 * n * sub
    return pl.pallas_call(
        functools.partial(back_kernel, n),
        out_shape=(
            jax.ShapeDtypeStruct((n, 2, sub, feat), bf16),
        )
        + (jax.ShapeDtypeStruct((size, width), bf16),) * n,
        grid=(width // tile,),
        in_specs=[
            pl.BlockSpec(memory_space=pltpu.SMEM),
            ANY,
            ANY,
            pl.BlockSpec((tile, feat), lambda i: (i, 0)),
        ]
        + [pl.BlockSpec((a.shape[0], tile), lambda i: (0, i)) for a in more]
        + [ANY] * len(after),
        out_specs=(
            pl.BlockSpec((n, 2, sub, feat), lambda i: (0, 0, 0, 0)),
        )
        + (pl.BlockSpec((size, tile), lambda i: (0, i)),) * n,
        scratch_shapes=[pltpu.SemaphoreType.DMA((2 * n,))],
        compiler_params=pltpu.CompilerParams(vmem_limit_bytes=VMEM),
        cost_estimate=cost(
            flops=2 * tokens * width * feat,
            bytes_accessed=2 * (2 * tokens * feat + width * feat + tokens * width),
            transcendentals=0,
        ),
    )(where, mine, other, w_down, *more, *after)


def masked_kernel(gate_ref, up_ref, keep_ref, *outs):
    for k in range(CHUNKS):
        gate = gate_ref[:, k].astype(f32)
        scale = keep_ref[:, k].astype(f32) * keep_scale
        value = gate * jax.nn.sigmoid(gate) * up_ref[:, k].astype(f32) * scale
        outs[k][...] = value.astype(bf16).reshape(outs[k].shape)


def masked(gate, up, keep):
    two, chunks, sub, width = gate.shape
    tile = width // 2 if width // 2 % 128 == 0 else width
    return pl.pallas_call(
        masked_kernel,
        out_shape=(jax.ShapeDtypeStruct((two * sub, width), bf16),) * chunks,
        grid=(width // tile,),
        in_specs=[pl.BlockSpec((two, chunks, sub, tile), lambda i: (0, 0, 0, i))] * 3,
        out_specs=(pl.BlockSpec((two * sub, tile), lambda i: (0, i)),) * chunks,
        compiler_params=pltpu.CompilerParams(vmem_limit_bytes=VMEM),
        cost_estimate=cost(
            flops=10 * gate.size, bytes_accessed=10 * gate.size, transcendentals=gate.size
        ),
    )(gate, up, keep)


def grads_kernel(n, *refs):
    parts = refs[:n]
    gate_ref, up_ref, keep_ref, weight_ref = refs[n : n + 4]
    out = refs[-1]
    total = parts[0][...].astype(f32)
    for part in parts[1:]:
        total = total + part[...].astype(f32)
    two, sub, tile = gate_ref.shape
    total = total.reshape(two, sub, tile)
    gate, up = gate_ref[...].astype(f32), up_ref[...].astype(f32)
    act = total * (keep_ref[...].astype(f32) * keep_scale * weight_ref[...])
    sig = jax.nn.sigmoid(gate)
    gpre = act * up * sig * (1.0 + gate * (1.0 - sig))
    out[0] = gpre.astype(bf16).reshape(out.shape[1:])
    out[1] = (act * gate * sig).astype(bf16).reshape(out.shape[1:])


def hidden_grads(k, parts, gate, up, keep, weights, after=()):
    n = len(parts)
    two, chunks, sub, width = gate.shape
    tile = width // 2 if width // 2 % 128 == 0 else width
    block = pl.BlockSpec((two, None, sub, tile), lambda i: (0, k, 0, i))
    size = two * sub * width
    return pl.pallas_call(
        functools.partial(grads_kernel, n),
        out_shape=jax.ShapeDtypeStruct((2, two * sub, width), bf16),
        grid=(width // tile,),
        in_specs=[pl.BlockSpec((two * sub, tile), lambda i: (0, i))] * n
        + [block] * 3
        + [pl.BlockSpec((two, None, sub, 1), lambda i: (0, k, 0, 0))]
        + [ANY] * len(after),
        out_specs=pl.BlockSpec((2, two * sub, tile), lambda i: (0, 0, i)),
        compiler_params=pltpu.CompilerParams(vmem_limit_bytes=VMEM),
        cost_estimate=cost(
            flops=20 * size, bytes_accessed=(12 + 2 * n) * size, transcendentals=size
        ),
    )(*parts, gate, up, keep, weights, *after)


def hidden_kernel(n, plan, count, where, *refs):
    slots, (wg_ref, wu_ref) = refs[:count], refs[count : count + 2]
    give_ref, keep_ref, left, sems = refs[-4:]

    @pl.when(pl.program_id(0) == 0)
    def _():
        copies = gather_slots(plan, slots, left, sems, 0)
        for copy in copies:
            copy.start()
        for copy in copies:
            copy.wait()

    half = len(plan) // 2
    width = left.shape[2]
    gpre = left[:half].reshape(-1, width)
    upre = left[half:].reshape(-1, width)
    part = over_width(gpre, wg_ref[...]) + over_width(upre, wu_ref[...])
    sub = give_ref.shape[1]
    part = part.reshape(n, 2, sub, part.shape[1])
    low = where[0] == 0
    for j in range(n):
        at = where[1 + j]
        keep_ref[at] = jnp.where(low, part[j, 0], part[j, 1])
        give_ref[at] = jnp.where(low, part[j, 1], part[j, 0]).astype(bf16)


def hidden(where, slots, plan, w_gate, w_up, n, after=()):
    size, width = slots[0].shape[1:]
    feat = w_gate.shape[0]
    tile = min(512, feat)
    tokens = len(plan) // 2 * size
    sub = tokens // (2 * n)
    return pl.pallas_call(
        functools.partial(hidden_kernel, n, plan, len(slots)),
        out_shape=(
            jax.ShapeDtypeStruct((n, sub, feat), bf16),
            jax.ShapeDtypeStruct((n, sub, feat), f32),
        ),
        grid=(feat // tile,),
        in_specs=[pl.BlockSpec(memory_space=pltpu.SMEM)]
        + [ANY] * len(slots)
        + [pl.BlockSpec((tile, width), lambda i: (i, 0))] * 2
        + [ANY] * len(after),
        out_specs=(pl.BlockSpec((n, sub, tile), lambda i: (0, 0, i)),) * 2,
        scratch_shapes=[
            pltpu.VMEM((len(plan), size, width), bf16),
            pltpu.SemaphoreType.DMA((len(plan),)),
        ],
        compiler_params=pltpu.CompilerParams(vmem_limit_bytes=VMEM),
        cost_estimate=cost(
            flops=4 * tokens * width * feat,
            bytes_accessed=4 * width * (tokens + feat) + 6 * n * sub * feat,
            transcendentals=0,
        ),
    )(where, *slots, w_gate, w_up, *after)


def down_grad_kernel(plan, count, weight_ref, *refs):
    drops, cots = refs[:count], refs[count : count + CHUNKS]
    out, left, right, sems = refs[-4:]
    step, tile = pl.program_id(0), out.shape[0]

    @pl.when(step == 0)
    def _():
        copies = gather_slots(plan, drops, left, sems, 0)
        for k in range(CHUNKS):
            copies.append(pltpu.make_async_copy(cots[k], right.at[k], sems.at[len(plan) + k]))
        for copy in copies:
            copy.start()
        for copy in copies:
            copy.wait()

    columns = pl.ds(pl.multiple_of(step * tile, tile), tile)
    a = left[:, :, columns].astype(f32) * weight_ref[...]
    a = a.astype(bf16).reshape(-1, tile)
    out[...] = over_tokens(a, right[...].reshape(a.shape[0], -1)).astype(bf16)


def down_grad(weights, drops, plan, cots, after=()):
    size, width = drops[0].shape
    feat = cots[0].shape[-1]
    tile = 256 if width % 256 == 0 else 128
    tokens = len(plan) * size
    return pl.pallas_call(
        functools.partial(down_grad_kernel, plan, len(drops)),
        out_shape=jax.ShapeDtypeStruct((width, feat), bf16),
        grid=(width // tile,),
        in_specs=[pl.BlockSpec((len(plan), size, 1), lambda i: (0, 0, 0))]
        + [ANY] * (len(drops) + len(cots) + len(after)),
        out_specs=pl.BlockSpec((tile, feat), lambda i: (i, 0)),
        scratch_shapes=[
            pltpu.VMEM((len(plan), size, width), bf16),
            pltpu.VMEM((CHUNKS,) + cots[0].shape, bf16),
            pltpu.SemaphoreType.DMA((len(plan) + CHUNKS,)),
        ],
        compiler_params=pltpu.CompilerParams(vmem_limit_bytes=VMEM),
        cost_estimate=cost(
            flops=2 * tokens * width * feat,
            bytes_accessed=2 * (tokens * feat + tokens * width + width * feat),
            transcendentals=0,
        ),
    )(weights, *drops, *cots, *after)


def per_device(
    stream_in, grad_out, gate_pre, up_pre, keep_mask, segment_ids, norm_gain, w_gate, w_up, w_down
):
    n_row = lax.axis_size("row")
    n_col = lax.axis_size("col")
    nz = n_col // 2
    tok_col, feat = stream_in.shape
    tok_row, width = gate_pre.shape
    total = tok_col * n_col
    sub = tok_col // CHUNKS
    col, row = lax.axis_index("col"), lax.axis_index("row")
    core, chip = lax.rem(col, 2), lax.div(col, 2)
    ring = [0] + list(range(1, nz, 2)) + list(range(nz - 2 + nz % 2, 0, -2))
    after_of = {ring[i]: ring[(i + 1) % nz] for i in range(nz)}

    def spots(chips):
        return jnp.stack([core] + [lax.bitwise_xor(c, row) for c in chips]).astype(jnp.int32)

    held = [sum(jnp.where(chip == ring[p], ring[(p - s) % nz], 0) for p in range(nz)) for s in range(nz)]
    around = spots(held)
    along = spots(range(nz))
    z_groups = [[2 * z + c for z in range(nz)] for c in range(2)]

    def swap(a):
        return lax.ppermute(a, "col", [(i, i ^ 1) for i in range(n_col)])

    def z_exchange(a):
        return lax.all_to_all(
            a, "col", split_axis=0, concat_axis=0, axis_index_groups=z_groups, tiled=True
        )

    def z_next(a):
        return lax.ppermute(a, "col", [(i, 2 * after_of[i // 2] + i % 2) for i in range(n_col)])

    def row_step(a, j):
        return lax.ppermute(a, "row", [(i, i ^ j) for i in range(n_row)])

    def near(a):
        return {j: row_step(a, j) for j in [1] + list(range(2, n_row, 2))}

    def far(got):
        return {k + 1: (row_step(a, k), row_step(b, 1)) for k, (a, b) in got.items()}

    def to_pass(got, after=()):
        first = pick(got[1], 0, after)
        return {k: (first, pick(got[k], 1, after)) for k in range(2, n_row, 2)}

    def all_slots(own, near_ones, far_ones):
        return [own] + list(near_ones.values()) + [a for two in far_ones.values() for a in two]

    nears, fars = [0, 1] + list(range(2, n_row, 2)), list(range(3, n_row, 2))

    def plan_of(half, base=0):
        return [
            (base + nears.index(j), half)
            if j in nears
            else (base + len(nears) + 2 * fars.index(j) + half, None)
            for j in range(n_row)
        ]

    def row_total(a):
        j = 1
        while j < n_row:
            a = a + row_step(a, j)
            j = 2 * j
        return a

    gate, up, keep = (a.reshape(2, CHUNKS, sub, width) for a in (gate_pre, up_pre, keep_mask))
    drop = masked(gate, up, keep)
    assert CHUNKS == 2
    drop_near = [near(a) for a in drop]
    drop_far = far({k: (drop_near[0][1], drop_near[1][k]) for k in range(2, n_row, 2)})
    drop_slots = [
        [drop[h]]
        + [drop_near[h][j] if j in drop_near[h] else drop_far[j][h] for j in range(1, n_row)]
        for h in range(CHUNKS)
    ]
    drops = drop_slots[0] + drop_slots[1]
    far_ones = [a for two in drop_far.values() for a in two]

    xs = stream_in.astype(f32)
    left_over = jnp.sum(xs * xs, axis=1)
    rows = [segment_ids.astype(f32)]
    for _ in range(3):
        rows.append(lax.reduce_precision(left_over, 8, 7))
        left_over = left_over - rows[-1]
    note = jnp.stack([jnp.pad(a, (0, width - a.shape[0])) for a in rows]).astype(bf16)
    note = jnp.pad(note, ((0, 12), (0, 0)))
    gain = norm_gain.reshape(1, feat)

    def read(notes):
        notes = jnp.stack([a[:4].astype(f32) for a in notes])
        onehot = (notes[:, 0, :tok_row, None] == jnp.arange(SEGS, dtype=f32)).astype(f32)
        counts = jnp.sum(onehot, axis=(0, 1))
        weights = jnp.sum(onehot * (total / (SEGS * counts)), axis=2)
        squares = jnp.sum(notes[:, 3, :tok_col] + notes[:, 2, :tok_col] + notes[:, 1, :tok_col], axis=0)
        recip = lax.rsqrt(squares / D + eps)
        return weights.reshape(n_row, 2, CHUNKS, sub), recip[:, None]

    def cot_gather(k, after):
        if k == 0:
            slots = [take(grad_out, 0, sub, 1, [drop[0]])[0]]
            for s in range(1, nz):
                slots.append(z_next(slots[-1]))
            return around, join(
                slots, [a for got in drop_near + [dict(enumerate(far_ones))] for a in got.values()]
            )
        return along, z_exchange(take(grad_out, k, sub, nz, after))

    cots, hids, hid_near, pairs, settled, slots = [], [], [], [], [], []
    plans = [[], []]
    plan = plan_of(0) + plan_of(1)

    def multiply(k, passed, after):
        mine = all_slots(hids[k], hid_near[k], far(passed))
        give, rest = hidden(along, mine, plan, w_gate, w_up, nz, after)
        for h in range(2):
            plans[h].extend(plan_of(h, len(slots)))
        slots.extend(mine)
        pairs.append(add_pair(rest, swap(give)))
        return give

    for k in range(CHUNKS):
        if k == 0:
            where, mine = cot_gather(0, [])
            other = swap(mine)
            late = []
        else:
            where, mine = along, z_exchange(take(grad_out, k, sub, nz, [other]))
            mine = hold(mine, [hids[-1]])
            other = swap(mine)
            passed = to_pass(hid_near[-1], [normed] if k == 1 else [])
            late = [a for two in passed.values() for a in two]
        cot, *partial = back(where, mine, other, w_down, [] if k else [note], late)
        cots.append(cot)
        parts = [partial[0]] + [row_step(partial[j], j) for j in range(1, n_row)]
        if k == 0:
            every, recip = read([a[2 * sub :] for a in parts])
            weights = every[0][:, :, :, None]
            all_weights = every.transpose(2, 0, 1, 3).reshape(CHUNKS * n_row, 2 * sub, 1)
            late = []
        else:
            late = [multiply(k - 1, passed, pairs[-1:])]
        hids.append(hidden_grads(k, parts, gate, up, keep, weights, late))
        hid_near.append(near(hids[k]))
        if k == 0:
            normed = normalize(stream_in, recip, gain, nz, [hids[0]])
            normed_mine = z_exchange(normed)
    order = [(i, None) for i in range(len(drops))]
    grad_down = down_grad(all_weights, drops, order, cots, [hids[-1]])
    multiply(CHUNKS - 1, to_pass(hid_near[-1], [grad_down]), pairs[-1:])
    normed_other = swap(normed_mine)
    for k in range(CHUNKS):
        late = []
        if k == CHUNKS - 1:
            grad_gate, grad_up = weight_grads(
                along,
                normed_mine,
                normed_other,
                slots,
                plans[0] + plans[1],
                pairs[-1:] + [s[1] for s in settled],
            )
            late = [grad_gate]
        settled.append(settle(k, z_exchange(pairs[k]), gain, stream_in, late))
    scaled = jnp.concatenate([s[0] for s in settled], axis=0)
    inner = jnp.concatenate([s[1] for s in settled], axis=0)
    inner = inner + sum(row_step(inner, j) for j in range(1, n_row))
    inner = inner[:, :1] / D
    branch = recip * (scaled - xs * (recip * recip * inner))
    grad_in = (grad_out.astype(f32) + branch).astype(bf16)
    return (grad_in, grad_gate, grad_up, grad_down)


def solution(mesh):
    return jax.shard_map(
        per_device,
        mesh=mesh,
        in_specs=(
            P("col", "row"),
            P("col", "row"),
            P("row", "col"),
            P("row", "col"),
            P("row", "col"),
            P("row"),
            P("row"),
            P("row", "col"),
            P("row", "col"),
            P("col", "row"),
        ),
        out_specs=(P("col", "row"), P("row", "col"), P("row", "col"), P("col", "row")),
        check_vma=False,
    )
```
